32 devices in a mesh: grp: 2 (over y), row: 4 (over z), col: 4 (over x, core).
Axes of the slice: x: 2, y: 2, z: 4, core: 2. Of those that a mesh axis runs over, the one named last changes fastest.
Arguments:
- pair: bfloat16 [512, 256, 128], P(('grp', 'row'), 'col'), parts along dimension 0, may hold values from -6 to 6
- cotangent: bfloat16 [512, 256, 128], P(('grp', 'row'), 'col'), parts along dimension 0, may hold values from -6 to 6
- tile_mask: int32 [4, 2], P('grp'), parts along dimension 0, may hold values 0 or 1
- chain_ids: int32 [512], P('grp'), parts along dimension 0, may hold values from 0 to 4, never falling along the last dimension, each value on 1 to 128 neighbouring positions
- gain_in: float32 [2, 128], replicated, may hold values from 0.1 to 1.9
- weight_in: bfloat16 [2, 128, 512], replicated, may hold values from -0.5 to 0.5
- weight_gate: bfloat16 [2, 128, 128], replicated, may hold values from -0.5 to 0.5
- gain_out: float32 [2, 128], replicated, may hold values from 0.1 to 1.9
- weight_out: bfloat16 [2, 128, 128], replicated, may hold values from -0.5 to 0.5
Outputs:
- grad_pair: bfloat16 [512, 256, 128], P(('grp', 'row'), 'col'), parts along dimension 0
- grad_weight_in: float32 [4, 128, 512], P('grp'), parts along dimension 0
- grad_weight_gate: float32 [4, 128, 128], P('grp'), parts along dimension 0
- grad_weight_out: float32 [4, 128, 128], P('grp'), parts along dimension 0
- grad_gain_in: float32 [4, 128], P('grp'), parts along dimension 0
- grad_gain_out: float32 [4, 128], P('grp'), parts along dimension 0
The draws below stay inside these ranges and needn't reach their ends.
There are 2 independent parts, one for each index of `grp`. The reference program is written for one: setup_inputs(seed, part) draws one part's arguments, and reference() takes and returns one part's arrays. A program takes and returns all parts, laid end to end along the dimension named above; an argument that names none is the same for every part. Nothing has to cross between parts.
Inputs may be any that keep to these rules, and one draw needn't show every extreme that they name: `chain_ids`: chain ids never fall along the tokens.
All inputs are finite; a program needn't handle non-finite values.
Results may differ from the reference program's by a relative error of at most 0.023.
Values may be sent and summed in bfloat16 or wider, within the bound.
A program may use at most 192 MiB of HBM per device.

```python
import math
import jax
import jax.numpy as jnp
import numpy as np
from jax import lax

TOKENS = 256
PAIR_DIM = 128
HIDDEN_SIZE = 128
TILE = 128
CHAINS = 5
TILES = 2


def plant(array, own_key, smallest, largest):
    shape = array.shape
    index_at = [jax.random.randint(jax.random.fold_in(own_key, axis), (), 0, shape[axis]) for axis in range(len(shape))]
    array = array.at[tuple(index_at)].set(smallest)
    longest = shape.index(max(shape))
    index_at[longest] = (index_at[longest] + 1) % shape[longest]
    return array.at[tuple(index_at)].set(largest)


def levels(stream_key, dims, pieces, smallest, high):
    def one(axis_at, shards_of):
        steps = jax.random.uniform(jax.random.fold_in(jax.random.fold_in(stream_key, 6), axis_at), (shards_of,), jnp.float32, smallest / len(pieces), high / len(pieces))
        return jnp.repeat(jnp.exp(steps), dims[axis_at] // shards_of).reshape((-1,) + (1,) * (len(dims) - axis_at - 1))

    loudness = one(*pieces[0])
    for cut in pieces[1:]:
        loudness = loudness * one(*cut)
    return loudness


def profile(number_of, total, limit, lean):
    loads = [(1 << 20) // math.isqrt(rank ** lean) + 1 for rank in range(2, number_of + 1)]
    surplus, counts = total - limit - (number_of - 1), [1] * (number_of - 1)
    while surplus > 0:
        candidates = [i for i in range(number_of - 1) if counts[i] < limit]
        mass, left = sum([loads[i] for i in candidates]), surplus
        for i in candidates:
            extra = min(limit - counts[i], max(1, left * loads[i] // mass), surplus)
            counts[i] = counts[i] + extra
            surplus = surplus - extra
    return np.array([limit] + counts)


def ragged_sizes(own_key, amount, total, most, skew):
    if amount == 2:
        one = jax.random.randint(own_key, (), max(1, total - most), min(most, total - 1) + 1)
        return jnp.stack([one, total - one])
    sizes = jnp.asarray(profile(amount, total, most, skew), jnp.int32)
    twos = (amount - 1) // 2
    donor, receiver = sizes[1:1 + 2 * twos:2], sizes[2:2 + 2 * twos:2]
    slack = jnp.minimum(donor - 1, most - receiver)
    passed = jax.random.randint(jax.random.fold_in(own_key, 1), (twos,), 0, 1 << 20) % (slack + 1)
    sizes = sizes.at[1:1 + 2 * twos:2].set(donor - passed).at[2:2 + 2 * twos:2].set(receiver + passed)
    return sizes[jax.random.permutation(jax.random.fold_in(own_key, 2), amount)]


def gaussian(own_key, extent, scale, bound, split=(), kind=jnp.bfloat16):
    drawn = jax.random.normal(own_key, extent, jnp.float32) * scale
    if len(split) > 0:
        drawn = levels(own_key, extent, split, -0.22, 0.18) * drawn
    return jnp.clip(drawn, min=-bound, max=bound).astype(kind)


def setup_inputs(seed: int = 0, part: int = 0) -> dict:
    keys = jax.random.split(jax.random.key(seed), 10)
    part_keys = jax.random.split(jax.random.fold_in(keys[9], part), 10)
    return {
        "pair": gaussian(part_keys[0], (TOKENS, TOKENS, PAIR_DIM), 1.0, 6.0, ((0, 4), (1, 4))),
        "cotangent": gaussian(part_keys[1], (TOKENS, TOKENS, PAIR_DIM), 1.0, 6.0, ((0, 4), (1, 4))),
        "tile_mask": plant((jax.random.randint(part_keys[2], (TILES, TILES), 0, 2) < 1).astype(jnp.int32), jax.random.fold_in(part_keys[2], 1), 0, 1),
        "chain_ids": jnp.searchsorted(jnp.cumsum(ragged_sizes(part_keys[3], CHAINS, TOKENS, TOKENS // 2, 2)), jnp.arange(TOKENS), side="right").astype(jnp.int32),
        "gain_in": jnp.clip(1.0 + 0.18 * jax.random.normal(keys[4], (2, PAIR_DIM), jnp.float32), 0.1, 1.9),
        "weight_in": gaussian(keys[5], (2, PAIR_DIM, 4 * HIDDEN_SIZE), PAIR_DIM ** -0.5, 0.5),
        "weight_gate": gaussian(keys[6], (2, PAIR_DIM, PAIR_DIM), PAIR_DIM ** -0.5, 0.5),
        "gain_out": jnp.clip(1.0 + 0.18 * jax.random.normal(keys[7], (2, HIDDEN_SIZE), jnp.float32), 0.1, 1.9),
        "weight_out": gaussian(keys[8], (2, HIDDEN_SIZE, PAIR_DIM), HIDDEN_SIZE ** -0.5, 0.5),
    }


eps = 1e-05

def layer_normalize(values):
    average = lax.optimization_barrier(jnp.mean(values, axis=-1, keepdims=True))
    centred = values - average
    inv_std = lax.rsqrt(lax.optimization_barrier(jnp.mean(centred * centred, axis=-1, keepdims=True)) + eps)
    return (centred * inv_std, inv_std)

def norm_backward_step(grad_hat, normed, inv_std):
    inner = lax.optimization_barrier(jnp.mean(grad_hat * normed, axis=-1, keepdims=True))
    return inv_std * (grad_hat - lax.optimization_barrier(jnp.mean(grad_hat, axis=-1, keepdims=True)) - normed * inner)

def front(flat_rows, pair_mask, gain_vector, weight_proj, weight_gating):
    zhat, inv_std = layer_normalize(flat_rows.astype(jnp.float32))
    znorm = (zhat * gain_vector).astype(jnp.bfloat16)
    projected = jnp.dot(znorm, weight_proj, preferred_element_type=jnp.float32)
    width = weight_proj.shape[1] // 4
    left_lin = projected[:, :width]
    left_gate = jax.nn.sigmoid(projected[:, width:2 * width])
    right_lin = projected[:, 2 * width:3 * width]
    right_gate = jax.nn.sigmoid(projected[:, 3 * width:])
    left_edge = (pair_mask[:, None] * left_gate * left_lin).astype(jnp.bfloat16)
    right_edge = (right_gate * right_lin).astype(jnp.bfloat16)
    gating = jax.nn.sigmoid(jnp.dot(znorm, weight_gating, preferred_element_type=jnp.float32))
    return (zhat, inv_std, znorm, left_lin, left_gate, right_lin, right_gate, left_edge, right_edge, gating)

def back_half(flat_rows, triangle_product, gating, gain_vector, weight_final):
    input_centred_scaled, input_inverse_deviation = layer_normalize(triangle_product)
    normalized_input = (input_centred_scaled * gain_vector).astype(jnp.bfloat16)
    triangle_update = jnp.dot(normalized_input, weight_final, preferred_element_type=jnp.float32)
    output_result = (flat_rows.astype(jnp.float32) + gating * triangle_update).astype(jnp.bfloat16)
    return (input_centred_scaled, input_inverse_deviation, normalized_input, triangle_update, output_result)

def post_grad(incoming, gating, backward_values, gain_vector, weight_final):
    input_centred_scaled, input_inverse_deviation, normalized_input, triangle_update = (backward_values[0], backward_values[1], backward_values[2], backward_values[3])
    grad_update = (incoming * gating).astype(jnp.bfloat16)
    grad_gating = (incoming * triangle_update * gating * (1.0 - gating)).astype(jnp.bfloat16)
    grad_wout = jnp.dot(normalized_input.T, grad_update, preferred_element_type=jnp.float32)
    gradient_normalized_input = jnp.dot(grad_update, weight_final.T, preferred_element_type=jnp.float32)
    gradient_gate_output = lax.optimization_barrier(jnp.sum(gradient_normalized_input * input_centred_scaled, axis=0))
    gradient_triangle = norm_backward_step(gradient_normalized_input * gain_vector, input_centred_scaled, input_inverse_deviation).astype(jnp.bfloat16)
    return (gradient_triangle, grad_gating, grad_wout, gradient_gate_output)

def pre_grad(incoming, grad_left, grad_right, grad_gating, front_vals, pair_mask, gain_vector, weight_proj, weight_gating):
    zhat, inv_std, znorm, left_lin, left_gate, right_lin, right_gate = front_vals[:7]
    masked = grad_left * pair_mask[:, None]
    grad_proj = jnp.concatenate([masked * left_gate, masked * left_lin * left_gate * (1.0 - left_gate), grad_right * right_gate, grad_right * right_lin * right_gate * (1.0 - right_gate)], axis=1).astype(jnp.bfloat16)
    grad_win = jnp.dot(znorm.T, grad_proj, preferred_element_type=jnp.float32)
    grad_wgate = jnp.dot(znorm.T, grad_gating, preferred_element_type=jnp.float32)
    grad_znorm = jnp.dot(grad_proj, weight_proj.T, preferred_element_type=jnp.float32)
    grad_znorm = grad_znorm + jnp.dot(grad_gating, weight_gating.T, preferred_element_type=jnp.float32)
    grad_gin = lax.optimization_barrier(jnp.sum(grad_znorm * zhat, axis=0))
    grad_input = incoming + norm_backward_step(grad_znorm * gain_vector, zhat, inv_std)
    return (grad_input, grad_win, grad_wgate, grad_gin)

def reference(pair, cotangent, tile_mask, chain_ids, gain_in, weight_in, weight_gate, gain_out, weight_out):
    tokens = pair.shape[0]
    channels = pair.shape[2]
    hidden = weight_out.shape[1]
    positions = jnp.arange(tokens, dtype=jnp.int32)
    tile_ids = (positions // TILE).astype(jnp.int32)
    tile_vals = tile_mask[tile_ids][:, tile_ids].astype(jnp.float32)
    same_chain = (chain_ids[:, None] == chain_ids[None, :]).astype(jnp.float32)
    pair_mask = jnp.maximum(tile_vals, same_chain).reshape(-1)
    shape_hid = (tokens, tokens, hidden)
    flat_one = pair.reshape(-1, channels)
    front_one = front(flat_one, pair_mask, gain_in[0], weight_in[0], weight_gate[0])
    left_one = front_one[7].reshape(shape_hid).astype(jnp.float32)
    right_one = front_one[8].reshape(shape_hid).astype(jnp.float32)
    tri_one = jnp.einsum('ikh,jkh->ijh', left_one, right_one).reshape(-1, hidden)
    back_one = back_half(flat_one, tri_one, front_one[9], gain_out[0], weight_out[0])
    flat_two = back_one[4]
    front_two = front(flat_two, pair_mask, gain_in[1], weight_in[1], weight_gate[1])
    left_two = front_two[7].reshape(shape_hid).astype(jnp.float32)
    right_two = front_two[8].reshape(shape_hid).astype(jnp.float32)
    tri_two = jnp.einsum('kih,kjh->ijh', left_two, right_two).reshape(-1, hidden)
    back_two = back_half(flat_two, tri_two, front_two[9], gain_out[1], weight_out[1])
    cot_two = cotangent.reshape(-1, channels).astype(jnp.float32)
    post_two = post_grad(cot_two, front_two[9], back_two, gain_out[1], weight_out[1])
    dtri_two = post_two[0].reshape(shape_hid).astype(jnp.float32)
    dleft_two = jnp.einsum('kjh,ijh->kih', right_two, dtri_two).reshape(-1, hidden)
    dright_two = jnp.einsum('kih,ijh->kjh', left_two, dtri_two).reshape(-1, hidden)
    pre_two = pre_grad(cot_two, dleft_two, dright_two, post_two[1], front_two, pair_mask, gain_in[1], weight_in[1], weight_gate[1])
    cot_one = lax.optimization_barrier(pre_two[0].astype(jnp.bfloat16)).astype(jnp.float32)
    post_one = post_grad(cot_one, front_one[9], back_one, gain_out[0], weight_out[0])
    dtri_one = post_one[0].reshape(shape_hid).astype(jnp.float32)
    dleft_one = jnp.einsum('ijh,jkh->ikh', dtri_one, right_one).reshape(-1, hidden)
    dright_one = jnp.einsum('ijh,ikh->jkh', dtri_one, left_one).reshape(-1, hidden)
    pre_one = pre_grad(cot_one, dleft_one, dright_one, post_one[1], front_one, pair_mask, gain_in[0], weight_in[0], weight_gate[0])
    factor = 1.0 / tokens
    grad_pair = pre_one[0].astype(jnp.bfloat16).reshape(tokens, tokens, channels)
    return (grad_pair, jnp.stack([pre_one[1], pre_two[1]]) * factor, jnp.stack([pre_one[2], pre_two[2]]) * factor, jnp.stack([post_one[2], post_two[2]]) * factor, jnp.stack([pre_one[3], pre_two[3]]) * factor, jnp.stack([post_one[3], post_two[3]]) * factor)
```

```python
import jax
import jax.numpy as jnp
from jax import lax
from jax.sharding import PartitionSpec as P

eps = 1e-05
axes = ("row", "col")


def contract(a, b, dim_a, dim_b):
    return lax.dot_general(a, b, (((dim_a,), (dim_b,)), ((), ())), preferred_element_type=jnp.float32)


def layer_normalize(values):
    average = jnp.mean(values, axis=0, keepdims=True)
    centred = values - average
    inv_std = lax.rsqrt(jnp.mean(centred * centred, axis=0, keepdims=True) + eps)
    return (centred * inv_std, inv_std)


def norm_backward_step(grad_hat, normed, inv_std):
    inner = jnp.mean(grad_hat * normed, axis=0, keepdims=True)
    return inv_std * (grad_hat - jnp.mean(grad_hat, axis=0, keepdims=True) - normed * inner)


def front(cells, pair_mask, gain, weight_proj, weight_gating):
    zhat, inv_std = layer_normalize(cells)
    znorm = (zhat * gain[:, None]).astype(jnp.bfloat16)
    projected = contract(weight_proj, znorm, 0, 0)
    width = weight_proj.shape[1] // 4
    left_lin = projected[:width]
    left_gate = jax.nn.sigmoid(projected[width : 2 * width])
    right_lin = projected[2 * width : 3 * width]
    right_gate = jax.nn.sigmoid(projected[3 * width :])
    left = (pair_mask * left_gate * left_lin).astype(jnp.bfloat16)
    right = (right_gate * right_lin).astype(jnp.bfloat16)
    gating = jax.nn.sigmoid(contract(weight_gating, znorm, 0, 0))
    return (zhat, inv_std, znorm, left_lin, left_gate, right_lin, right_gate, left, right, gating)


def back_half(cells, tri, gating, gain, weight_final):
    xhat, inv_std = layer_normalize(tri)
    xnorm = (xhat * gain[:, None]).astype(jnp.bfloat16)
    update = contract(weight_final, xnorm, 0, 0)
    result = (cells + gating * update).astype(jnp.bfloat16)
    return (xhat, inv_std, xnorm, update, result)


def post_grad(incoming, gating, backs, gain, weight_final):
    xhat, inv_std, xnorm, update = backs[:4]
    grad_update = (incoming * gating).astype(jnp.bfloat16)
    grad_gating = (incoming * update * gating * (1.0 - gating)).astype(jnp.bfloat16)
    grad_wout = contract(xnorm, grad_update, 1, 1)
    grad_xnorm = contract(weight_final, grad_update, 1, 0)
    grad_gout = jnp.sum(grad_xnorm * xhat, axis=1)
    grad_tri = norm_backward_step(grad_xnorm * gain[:, None], xhat, inv_std).astype(jnp.bfloat16)
    return (grad_tri, grad_gating, grad_wout, grad_gout)


def pre_grad(
    incoming, grad_left, grad_right, grad_gating, fronts, pair_mask, gain, weight_proj, weight_gating
):
    zhat, inv_std, znorm, left_lin, left_gate, right_lin, right_gate = fronts[:7]
    masked = grad_left * pair_mask
    grad_proj = jnp.concatenate(
        [
            masked * left_gate,
            masked * left_lin * left_gate * (1.0 - left_gate),
            grad_right * right_gate,
            grad_right * right_lin * right_gate * (1.0 - right_gate),
        ],
        axis=0,
    ).astype(jnp.bfloat16)
    grad_win = contract(znorm, grad_proj, 1, 1)
    grad_wgate = contract(znorm, grad_gating, 1, 1)
    grad_znorm = contract(weight_proj, grad_proj, 1, 0)
    grad_znorm = grad_znorm + contract(weight_gating, grad_gating, 1, 0)
    grad_gin = jnp.sum(grad_znorm * zhat, axis=1)
    grad_input = incoming + norm_backward_step(grad_znorm * gain[:, None], zhat, inv_std)
    return (grad_input, grad_win, grad_wgate, grad_gin)


def local_mask(tile_mask, chain_ids, row_start, col_start, rows_dev, cols_dev):
    tile_count = tile_mask.shape[0]
    tile_size = chain_ids.shape[0] // tile_count
    row_ids = row_start + jnp.arange(rows_dev, dtype=jnp.int32)
    col_ids = col_start + jnp.arange(cols_dev, dtype=jnp.int32)
    tile_index = jnp.arange(tile_count, dtype=jnp.int32)
    row_hot = (row_ids[:, None] // tile_size == tile_index[None, :]).astype(jnp.float32)
    col_hot = (col_ids[:, None] // tile_size == tile_index[None, :]).astype(jnp.float32)
    tile_vals = jnp.dot(jnp.dot(row_hot, tile_mask.astype(jnp.float32)), col_hot.T)
    row_chain = lax.dynamic_slice_in_dim(chain_ids, row_start, rows_dev)
    col_chain = lax.dynamic_slice_in_dim(chain_ids, col_start, cols_dev)
    same_chain = (row_chain[:, None] == col_chain[None, :]).astype(jnp.float32)
    return jnp.maximum(tile_vals, same_chain).reshape(1, -1)


def per_device(
    pair, cotangent, tile_mask, chain_ids, gain_in, weight_in, weight_gate, gain_out, weight_out
):
    rows_dev, cols_dev, channels = pair.shape
    hidden = weight_out.shape[1]
    grid_rows, grid_cols = lax.axis_size("row"), lax.axis_size("col")
    peers = grid_rows * grid_cols
    share = hidden // peers
    tokens = rows_dev * grid_rows
    cells_dev = rows_dev * cols_dev

    def exchange(blocks):
        return lax.all_to_all(blocks, axes, 0, 0)

    def to_channels(*arrays):
        sent = jnp.concatenate([a.reshape(peers, share, cells_dev) for a in arrays], axis=1)
        got = exchange(sent).reshape(grid_rows, grid_cols, len(arrays) * share, rows_dev, cols_dev)
        whole = got.transpose(2, 0, 3, 1, 4).reshape(len(arrays) * share, tokens, tokens)
        return [whole[n * share : (n + 1) * share] for n in range(len(arrays))]

    def to_cells(*arrays):
        stacked = jnp.concatenate([a.astype(jnp.bfloat16) for a in arrays], axis=0)
        split = stacked.reshape(-1, grid_rows, rows_dev, grid_cols, cols_dev)
        sent = split.transpose(1, 3, 0, 2, 4).reshape(peers, -1, cells_dev)
        got = exchange(sent).reshape(peers, len(arrays), share, cells_dev)
        return [got[:, n].reshape(hidden, cells_dev).astype(jnp.float32) for n in range(len(arrays))]

    def triangle(spec, a, b):
        return jnp.einsum(spec, a, b, preferred_element_type=jnp.float32)

    row_start = lax.axis_index("row") * rows_dev
    col_start = lax.axis_index("col") * cols_dev
    pair_mask = local_mask(tile_mask, chain_ids, row_start, col_start, rows_dev, cols_dev)
    cells_one = pair.reshape(-1, channels).T.astype(jnp.float32)
    front_one = front(cells_one, pair_mask, gain_in[0], weight_in[0], weight_gate[0])
    left_one, right_one = to_channels(front_one[7], front_one[8])
    (tri_one,) = to_cells(triangle("hik,hjk->hij", left_one, right_one))
    back_one = back_half(cells_one, tri_one, front_one[9], gain_out[0], weight_out[0])
    cells_two = back_one[4].astype(jnp.float32)
    front_two = front(cells_two, pair_mask, gain_in[1], weight_in[1], weight_gate[1])
    left_two, right_two = to_channels(front_two[7], front_two[8])
    (tri_two,) = to_cells(triangle("hki,hkj->hij", left_two, right_two))
    back_two = back_half(cells_two, tri_two, front_two[9], gain_out[1], weight_out[1])
    cot_two = cotangent.reshape(-1, channels).T.astype(jnp.float32)
    post_two = post_grad(cot_two, front_two[9], back_two, gain_out[1], weight_out[1])
    (dtri_two,) = to_channels(post_two[0])
    dleft_two, dright_two = to_cells(
        triangle("hkj,hij->hki", right_two, dtri_two), triangle("hki,hij->hkj", left_two, dtri_two)
    )
    pre_two = pre_grad(
        cot_two,
        dleft_two,
        dright_two,
        post_two[1],
        front_two,
        pair_mask,
        gain_in[1],
        weight_in[1],
        weight_gate[1],
    )
    cot_one = pre_two[0].astype(jnp.bfloat16).astype(jnp.float32)
    post_one = post_grad(cot_one, front_one[9], back_one, gain_out[0], weight_out[0])
    (dtri_one,) = to_channels(post_one[0])
    dleft_one, dright_one = to_cells(
        triangle("hij,hjk->hik", dtri_one, right_one), triangle("hij,hik->hjk", dtri_one, left_one)
    )
    pre_one = pre_grad(
        cot_one,
        dleft_one,
        dright_one,
        post_one[1],
        front_one,
        pair_mask,
        gain_in[0],
        weight_in[0],
        weight_gate[0],
    )
    grad_pair = pre_one[0].astype(jnp.bfloat16).T.reshape(rows_dev, cols_dev, channels)

    factor = 1.0 / tokens
    pieces = []
    for pre, post in ((pre_one, post_one), (pre_two, post_two)):
        pieces += [pre[1][:, n * hidden : (n + 1) * hidden] for n in range(4)] + [pre[2], post[2].T]
    pieces += [pre_one[3][None], pre_two[3][None], post_one[3][None], post_two[3][None]]
    stacked = jnp.concatenate(pieces, axis=0) * factor
    rows = stacked.shape[0]
    padded = jnp.pad(stacked, ((0, -rows % peers), (0, 0))).astype(jnp.bfloat16)
    parts = exchange(padded.reshape(peers, -1, channels))
    summed = jnp.sum(parts.astype(jnp.float32), axis=0).astype(jnp.bfloat16)
    totals = exchange(jnp.broadcast_to(summed, (peers,) + summed.shape))
    totals = totals.reshape(-1, channels)[:rows].astype(jnp.float32)
    blocks = totals[: 12 * channels].reshape(2, 6, channels, channels)
    gains = totals[12 * channels :]
    return (
        grad_pair,
        jnp.concatenate([blocks[:, n] for n in range(4)], axis=2),
        blocks[:, 4],
        blocks[:, 5].transpose(0, 2, 1),
        gains[:2],
        gains[2:4],
    )


def solution(mesh):
    in_specs = (
        P(("grp", "row"), "col", None),
        P(("grp", "row"), "col", None),
        P("grp", None),
        P("grp"),
        P(),
        P(),
        P(),
        P(),
        P(),
    )
    out_specs = (
        P(("grp", "row"), "col", None),
        P("grp", None, None),
        P("grp", None, None),
        P("grp", None, None),
        P("grp", None),
        P("grp", None),
    )
    return jax.shard_map(
        per_device, mesh=mesh, in_specs=in_specs, out_specs=out_specs, check_vma=False
    )
```

```python
import functools

import jax
import jax.numpy as jnp
from jax import lax
from jax.experimental import pallas as pl
from jax.experimental.pallas import tpu as pltpu
from jax.sharding import PartitionSpec as P

eps = 1e-05
axes = ("row", "col")


def contract(a, b, dim_a, dim_b):
    return lax.dot_general(a, b, (((dim_a,), (dim_b,)), ((), ())), preferred_element_type=jnp.float32)


def layer_normalize(values):
    average = jnp.mean(values, axis=0, keepdims=True)
    centred = values - average
    inv_std = lax.rsqrt(jnp.mean(centred * centred, axis=0, keepdims=True) + eps)
    return (centred * inv_std, inv_std)


def norm_backward_step(grad_hat, normed, inv_std):
    inner = jnp.mean(grad_hat * normed, axis=0, keepdims=True)
    return inv_std * (grad_hat - jnp.mean(grad_hat, axis=0, keepdims=True) - normed * inner)


def front(cells, pair_mask, gain, weight_proj, weight_gating):
    zhat, inv_std = layer_normalize(cells)
    znorm = (zhat * gain[:, None]).astype(jnp.bfloat16)
    projected = contract(weight_proj, znorm, 0, 0)
    width = weight_proj.shape[1] // 4
    left_lin = projected[:width]
    left_gate = jax.nn.sigmoid(projected[width : 2 * width])
    right_lin = projected[2 * width : 3 * width]
    right_gate = jax.nn.sigmoid(projected[3 * width :])
    left = (pair_mask * left_gate * left_lin).astype(jnp.bfloat16)
    right = (right_gate * right_lin).astype(jnp.bfloat16)
    gating = jax.nn.sigmoid(contract(weight_gating, znorm, 0, 0))
    return (zhat, inv_std, znorm, left_lin, left_gate, right_lin, right_gate, left, right, gating)


def back_half(cells, tri, gating, gain, weight_final):
    xhat, inv_std = layer_normalize(tri)
    xnorm = (xhat * gain[:, None]).astype(jnp.bfloat16)
    update = contract(weight_final, xnorm, 0, 0)
    result = (cells + gating * update).astype(jnp.bfloat16)
    return (xhat, inv_std, xnorm, update, result)


def post_grad(incoming, gating, backs, gain, weight_final):
    xhat, inv_std, xnorm, update = backs[:4]
    grad_update = (incoming * gating).astype(jnp.bfloat16)
    grad_gating = (incoming * update * gating * (1.0 - gating)).astype(jnp.bfloat16)
    grad_wout = contract(xnorm, grad_update, 1, 1)
    grad_xnorm = contract(weight_final, grad_update, 1, 0)
    grad_gout = jnp.sum(grad_xnorm * xhat, axis=1)
    grad_tri = norm_backward_step(grad_xnorm * gain[:, None], xhat, inv_std).astype(jnp.bfloat16)
    return (grad_tri, grad_gating, grad_wout, grad_gout)


def pre_grad(
    incoming, grad_left, grad_right, grad_gating, fronts, pair_mask, gain, weight_proj, weight_gating
):
    zhat, inv_std, znorm, left_lin, left_gate, right_lin, right_gate = fronts[:7]
    masked = grad_left * pair_mask
    grad_proj = jnp.concatenate(
        [
            masked * left_gate,
            masked * left_lin * left_gate * (1.0 - left_gate),
            grad_right * right_gate,
            grad_right * right_lin * right_gate * (1.0 - right_gate),
        ],
        axis=0,
    ).astype(jnp.bfloat16)
    grad_win = contract(znorm, grad_proj, 1, 1)
    grad_wgate = contract(znorm, grad_gating, 1, 1)
    grad_znorm = contract(weight_proj, grad_proj, 1, 0)
    grad_znorm = grad_znorm + contract(weight_gating, grad_gating, 1, 0)
    grad_gin = jnp.sum(grad_znorm * zhat, axis=1)
    grad_input = incoming + norm_backward_step(grad_znorm * gain[:, None], zhat, inv_std)
    return (grad_input, grad_win, grad_wgate, grad_gin)


lanes = 128
half = lanes // 2


def swap_halves(even, odd):
    low = lax.broadcasted_iota(jnp.int32, even.shape, 1) < half
    return (
        jnp.where(low, even, pltpu.roll(odd, half, 1)),
        jnp.where(low, pltpu.roll(even, half, 1), odd),
    )


def unpack(x_ref, rows_ref):
    chunks = x_ref.shape[2] // lanes

    def step(p, _):
        for m in range(chunks):
            rows_ref[p, m * 16 : (m + 1) * 16, :] = x_ref[
                p, :, m * lanes : (m + 1) * lanes
            ].astype(jnp.float32)
        return 0

    lax.fori_loop(0, x_ref.shape[0], step, 0)


def pack(rows_ref, o_ref):
    chunks = o_ref.shape[2] // lanes

    def step(p, _):
        for m in range(chunks):
            o_ref[p, :, m * lanes : (m + 1) * lanes] = rows_ref[
                p, m * 16 : (m + 1) * 16, :
            ].astype(jnp.bfloat16)
        return 0

    lax.fori_loop(0, o_ref.shape[0], step, 0)


def row_sets(rows_ref, first, split):
    pairs = rows_ref.shape[1] // 16
    if split:
        return [pl.ds(first, pairs, stride=16), pl.ds(first + 8, pairs, stride=16)]
    return [pl.ds(first, pairs, stride=16)]


def gather_matrix(rows_ref, first, split, whole_ref, sides):
    grid_rows, grid_cols = sides
    for r in range(grid_rows):
        for c in range(grid_cols // 2):
            p = r * grid_cols + 2 * c
            sets = row_sets(rows_ref, first, split)
            a = jnp.concatenate([rows_ref[p, s, :] for s in sets], axis=0)
            b = jnp.concatenate([rows_ref[p + 1, s, :] for s in sets], axis=0)
            even, odd = swap_halves(a, b)
            rows = even.shape[0]
            whole_ref[c, pl.ds(2 * rows * r, rows, stride=2), :] = even
            whole_ref[c, pl.ds(2 * rows * r + 1, rows, stride=2), :] = odd
    return jnp.concatenate(
        [whole_ref[c].astype(jnp.bfloat16) for c in range(grid_cols // 2)], axis=1
    )


def scatter_matrix(values, whole_ref, rows_ref, first, split, sides):
    grid_rows, grid_cols = sides
    rows = values.shape[0] // grid_rows // 2
    for c in range(grid_cols // 2):
        whole_ref[c] = values[:, c * lanes : (c + 1) * lanes]
    for r in range(grid_rows):
        for c in range(grid_cols // 2):
            p = r * grid_cols + 2 * c
            even = whole_ref[c, pl.ds(2 * rows * r, rows, stride=2), :]
            odd = whole_ref[c, pl.ds(2 * rows * r + 1, rows, stride=2), :]
            blocks = swap_halves(even, odd)
            sets = row_sets(rows_ref, first, split)
            size = rows // len(sets)
            for n in range(2):
                for k, s in enumerate(sets):
                    rows_ref[p + n, s, :] = blocks[n][k * size : (k + 1) * size]


def forward_kernel(dims, sides, x_ref, o_ref, left_ref, right_ref, rows_in, rows_out, whole, whole2):
    unpack(x_ref, rows_in)

    def step(h, _):
        left = gather_matrix(rows_in, h, False, whole.at[0], sides)
        right = gather_matrix(rows_in, h + 8, False, whole.at[1], sides)
        left_ref[h] = left
        right_ref[h] = right
        scatter_matrix(contract(left, right, *dims), whole2.at[0], rows_out, h, True, sides)
        return 0

    lax.fori_loop(0, left_ref.shape[0], step, 0)
    pack(rows_out, o_ref)


def backward_kernel(
    outgoing, sides, x_ref, left_ref, right_ref, o_ref, rows_in, rows_out, whole, whole2
):
    unpack(x_ref, rows_in)

    def step(h, _):
        grad = gather_matrix(rows_in, h, True, whole.at[0], sides)
        left, right = left_ref[h], right_ref[h]
        if outgoing:
            grad_left, grad_right = contract(grad, right, 1, 0), contract(grad, left, 0, 0)
        else:
            grad_left, grad_right = contract(right, grad, 1, 1), contract(left, grad, 1, 0)
        scatter_matrix(grad_left, whole2.at[0], rows_out, h, False, sides)
        scatter_matrix(grad_right, whole2.at[1], rows_out, h + 8, False, sides)
        return 0

    lax.fori_loop(0, left_ref.shape[0], step, 0)
    pack(rows_out, o_ref)


def triangle_call(body, operands, out_shapes, peers, tokens, big_in, cells):
    wide, narrow = (peers, cells // lanes * 16, lanes), (peers, cells // lanes * 8, lanes)
    vmem = pl.BlockSpec(memory_space=pltpu.VMEM)
    square = pltpu.VMEM((2, tokens // lanes, tokens, lanes), jnp.float32)
    return pl.pallas_call(
        body,
        out_shape=out_shapes,
        in_specs=[vmem] * len(operands),
        out_specs=[vmem] * len(out_shapes),
        scratch_shapes=[
            pltpu.VMEM(wide if big_in else narrow, jnp.float32),
            pltpu.VMEM(narrow if big_in else wide, jnp.float32),
            square,
            square,
        ],
        compiler_params=pltpu.CompilerParams(vmem_limit_bytes=40 << 20),
    )(*operands)


def local_mask(tile_mask, chain_ids, row_start, col_start, rows_dev, cols_dev):
    tile_count = tile_mask.shape[0]
    tile_size = chain_ids.shape[0] // tile_count
    row_ids = row_start + jnp.arange(rows_dev, dtype=jnp.int32)
    col_ids = col_start + jnp.arange(cols_dev, dtype=jnp.int32)
    tile_index = jnp.arange(tile_count, dtype=jnp.int32)
    row_hot = (row_ids[:, None] // tile_size == tile_index[None, :]).astype(jnp.float32)
    col_hot = (col_ids[:, None] // tile_size == tile_index[None, :]).astype(jnp.float32)
    tile_vals = jnp.dot(jnp.dot(row_hot, tile_mask.astype(jnp.float32)), col_hot.T)
    row_chain = lax.dynamic_slice_in_dim(chain_ids, row_start, rows_dev)
    col_chain = lax.dynamic_slice_in_dim(chain_ids, col_start, cols_dev)
    same_chain = (row_chain[:, None] == col_chain[None, :]).astype(jnp.float32)
    return jnp.maximum(tile_vals, same_chain).reshape(1, -1)


def per_device(
    pair, cotangent, tile_mask, chain_ids, gain_in, weight_in, weight_gate, gain_out, weight_out
):
    rows_dev, cols_dev, channels = pair.shape
    hidden = weight_out.shape[1]
    grid_rows, grid_cols = lax.axis_size("row"), lax.axis_size("col")
    peers = grid_rows * grid_cols
    share = hidden // peers
    tokens = rows_dev * grid_rows
    cells_dev = rows_dev * cols_dev

    def exchange(blocks):
        return lax.all_to_all(blocks, axes, 0, 0)

    def triangle(spec, a, b):
        return jnp.einsum(spec, a, b, preferred_element_type=jnp.float32)

    kernels = share == 8 and cols_dev == half and rows_dev == half and grid_cols % 2 == 0
    sides = (grid_rows, grid_cols)
    whole_grid = (share, tokens, tokens)

    def spread(*arrays):
        sent = [a.reshape(peers, share, cells_dev) for a in arrays]
        if len(arrays) == 2 or not kernels:
            return exchange(jnp.concatenate(sent, axis=1))
        halves = sent[0].reshape(peers, share, 2, -1).transpose(0, 2, 1, 3)
        return exchange(halves.reshape(peers, 2 * share, -1))

    def collect(blocks, count):
        got = exchange(blocks).astype(jnp.float32)
        if count == 1 and kernels:
            got = got.reshape(peers, 2, share, -1).transpose(0, 2, 1, 3)
            return [got.reshape(hidden, cells_dev)]
        got = got.reshape(peers, count, share, cells_dev)
        return [got[:, n].reshape(hidden, cells_dev) for n in range(count)]

    def assemble(got, count):
        got = got.reshape(grid_rows, grid_cols, count * share, rows_dev, cols_dev)
        whole = got.transpose(2, 0, 3, 1, 4).reshape(count * share, tokens, tokens)
        return [whole[n * share : (n + 1) * share] for n in range(count)]

    def divide(*arrays):
        stacked = jnp.concatenate([a.astype(jnp.bfloat16) for a in arrays], axis=0)
        split = stacked.reshape(-1, grid_rows, rows_dev, grid_cols, cols_dev)
        return split.transpose(1, 3, 0, 2, 4).reshape(peers, -1, cells_dev)

    def shapes(*dims):
        return [jax.ShapeDtypeStruct(d, jnp.bfloat16) for d in dims]

    def forward_triangle(left, right, outgoing):
        got = spread(left, right)
        if kernels:
            dims = (1, 1) if outgoing else (0, 0)
            blocks, left_all, right_all = triangle_call(
                functools.partial(forward_kernel, dims, sides),
                [got],
                shapes((peers, 16, cells_dev // 2), whole_grid, whole_grid),
                peers,
                tokens,
                True,
                cells_dev,
            )
        else:
            left_all, right_all = assemble(got, 2)
            spec = "hik,hjk->hij" if outgoing else "hki,hkj->hij"
            blocks = divide(triangle(spec, left_all, right_all))
        return collect(blocks, 1)[0], left_all, right_all

    def backward_triangle(grad, left_all, right_all, outgoing):
        got = spread(grad)
        if kernels:
            (blocks,) = triangle_call(
                functools.partial(backward_kernel, outgoing, sides),
                [got, left_all, right_all],
                shapes((peers, 16, cells_dev)),
                peers,
                tokens,
                False,
                cells_dev,
            )
        else:
            (whole,) = assemble(got, 1)
            if outgoing:
                grads = ("hij,hjk->hik", whole, right_all), ("hij,hik->hjk", whole, left_all)
            else:
                grads = ("hkj,hij->hki", right_all, whole), ("hki,hij->hkj", left_all, whole)
            blocks = divide(*[triangle(*g) for g in grads])
        return collect(blocks, 2)

    row_start = lax.axis_index("row") * rows_dev
    col_start = lax.axis_index("col") * cols_dev
    pair_mask = local_mask(tile_mask, chain_ids, row_start, col_start, rows_dev, cols_dev)
    cells_one = pair.reshape(-1, channels).T.astype(jnp.float32)
    front_one = front(cells_one, pair_mask, gain_in[0], weight_in[0], weight_gate[0])
    tri_one, left_one, right_one = forward_triangle(front_one[7], front_one[8], True)
    back_one = back_half(cells_one, tri_one, front_one[9], gain_out[0], weight_out[0])
    cells_two = back_one[4].astype(jnp.float32)
    front_two = front(cells_two, pair_mask, gain_in[1], weight_in[1], weight_gate[1])
    tri_two, left_two, right_two = forward_triangle(front_two[7], front_two[8], False)
    back_two = back_half(cells_two, tri_two, front_two[9], gain_out[1], weight_out[1])
    cot_two = cotangent.reshape(-1, channels).T.astype(jnp.float32)
    post_two = post_grad(cot_two, front_two[9], back_two, gain_out[1], weight_out[1])
    dleft_two, dright_two = backward_triangle(post_two[0], left_two, right_two, False)
    pre_two = pre_grad(
        cot_two,
        dleft_two,
        dright_two,
        post_two[1],
        front_two,
        pair_mask,
        gain_in[1],
        weight_in[1],
        weight_gate[1],
    )
    cot_one = pre_two[0].astype(jnp.bfloat16).astype(jnp.float32)
    post_one = post_grad(cot_one, front_one[9], back_one, gain_out[0], weight_out[0])
    dleft_one, dright_one = backward_triangle(post_one[0], left_one, right_one, True)
    pre_one = pre_grad(
        cot_one,
        dleft_one,
        dright_one,
        post_one[1],
        front_one,
        pair_mask,
        gain_in[0],
        weight_in[0],
        weight_gate[0],
    )
    grad_pair = pre_one[0].astype(jnp.bfloat16).T.reshape(rows_dev, cols_dev, channels)

    factor = 1.0 / tokens
    pieces = []
    for pre, post in ((pre_one, post_one), (pre_two, post_two)):
        pieces += [pre[1][:, n * hidden : (n + 1) * hidden] for n in range(4)] + [pre[2], post[2]]
    pieces += [pre_one[3][None], pre_two[3][None], post_one[3][None], post_two[3][None]]
    stacked = jnp.concatenate(pieces, axis=0) * factor
    rows = stacked.shape[0]
    padded = jnp.pad(stacked, ((0, -rows % peers), (0, 0))).astype(jnp.bfloat16)
    parts = exchange(padded.reshape(peers, -1, channels))
    summed = jnp.sum(parts.astype(jnp.float32), axis=0).astype(jnp.bfloat16)
    totals = exchange(jnp.broadcast_to(summed, (peers,) + summed.shape))
    totals = totals.reshape(-1, channels)[:rows].astype(jnp.float32)
    blocks = totals[: 12 * channels].reshape(2, 6, channels, channels)
    gains = totals[12 * channels :]
    return (
        grad_pair,
        jnp.concatenate([blocks[:, n] for n in range(4)], axis=2),
        blocks[:, 4],
        blocks[:, 5],
        gains[:2],
        gains[2:4],
    )


def solution(mesh):
    in_specs = (
        P(("grp", "row"), "col", None),
        P(("grp", "row"), "col", None),
        P("grp", None),
        P("grp"),
        P(),
        P(),
        P(),
        P(),
        P(),
    )
    out_specs = (
        P(("grp", "row"), "col", None),
        P("grp", None, None),
        P("grp", None, None),
        P("grp", None, None),
        P("grp", None),
        P("grp", None),
    )
    return jax.shard_map(
        per_device, mesh=mesh, in_specs=in_specs, out_specs=out_specs, check_vma=False
    )
```

```python
import functools

import jax
import jax.numpy as jnp
from jax import lax
from jax.experimental import pallas as pl
from jax.experimental.pallas import tpu as pltpu
from jax.sharding import PartitionSpec as P

eps = 1e-05
axes = ("row", "col")


def contract(a, b, dim_a, dim_b):
    return lax.dot_general(a, b, (((dim_a,), (dim_b,)), ((), ())), preferred_element_type=jnp.float32)


def layer_normalize(values):
    average = jnp.mean(values, axis=0, keepdims=True)
    centred = values - average
    inv_std = lax.rsqrt(jnp.mean(centred * centred, axis=0, keepdims=True) + eps)
    return (centred * inv_std, inv_std)


def norm_backward_step(grad_hat, normed, inv_std):
    inner = jnp.mean(grad_hat * normed, axis=0, keepdims=True)
    return inv_std * (grad_hat - jnp.mean(grad_hat, axis=0, keepdims=True) - normed * inner)


def front(cells, pair_mask, gain, weight_proj, weight_gating):
    zhat, inv_std = layer_normalize(cells)
    znorm = (zhat * gain[:, None]).astype(jnp.bfloat16)
    projected = contract(weight_proj, znorm, 0, 0)
    width = weight_proj.shape[1] // 4
    left_lin = projected[:width]
    left_gate = jax.nn.sigmoid(projected[width : 2 * width])
    right_lin = projected[2 * width : 3 * width]
    right_gate = jax.nn.sigmoid(projected[3 * width :])
    left = (pair_mask * left_gate * left_lin).astype(jnp.bfloat16)
    right = (right_gate * right_lin).astype(jnp.bfloat16)
    gating = jax.nn.sigmoid(contract(weight_gating, znorm, 0, 0))
    return (zhat, inv_std, znorm, left_lin, left_gate, right_lin, right_gate, left, right, gating)


def back_half(cells, tri, gating, gain, weight_final):
    xhat, inv_std = layer_normalize(tri)
    xnorm = (xhat * gain[:, None]).astype(jnp.bfloat16)
    update = contract(weight_final, xnorm, 0, 0)
    result = (cells + gating * update).astype(jnp.bfloat16)
    return (xhat, inv_std, xnorm, update, result)


def post_grad(incoming, gating, backs, gain, weight_final):
    xhat, inv_std, xnorm, update = backs[:4]
    grad_update = (incoming * gating).astype(jnp.bfloat16)
    grad_gating = (incoming * update * gating * (1.0 - gating)).astype(jnp.bfloat16)
    grad_wout = contract(xnorm, grad_update, 1, 1)
    grad_xnorm = contract(weight_final, grad_update, 1, 0)
    grad_gout = jnp.sum(grad_xnorm * xhat, axis=1)
    grad_tri = norm_backward_step(grad_xnorm * gain[:, None], xhat, inv_std).astype(jnp.bfloat16)
    return (grad_tri, grad_gating, grad_wout, grad_gout)


def pre_grad(
    incoming, grad_left, grad_right, grad_gating, fronts, pair_mask, gain, weight_proj, weight_gating
):
    zhat, inv_std, znorm, left_lin, left_gate, right_lin, right_gate = fronts[:7]
    masked = grad_left * pair_mask
    grad_proj = jnp.concatenate(
        [
            masked * left_gate,
            masked * left_lin * left_gate * (1.0 - left_gate),
            grad_right * right_gate,
            grad_right * right_lin * right_gate * (1.0 - right_gate),
        ],
        axis=0,
    ).astype(jnp.bfloat16)
    grad_win = contract(znorm, grad_proj, 1, 1)
    grad_wgate = contract(znorm, grad_gating, 1, 1)
    grad_znorm = contract(weight_proj, grad_proj, 1, 0)
    grad_znorm = grad_znorm + contract(weight_gating, grad_gating, 1, 0)
    grad_gin = jnp.sum(grad_znorm * zhat, axis=1)
    grad_input = incoming + norm_backward_step(grad_znorm * gain[:, None], zhat, inv_std)
    return (grad_input, grad_win, grad_wgate, grad_gin)


lanes = 128
half = lanes // 2


def swap_halves(even, odd):
    low = lax.broadcasted_iota(jnp.int32, even.shape, 1) < half
    return (
        jnp.where(low, even, pltpu.roll(odd, half, 1)),
        jnp.where(low, pltpu.roll(even, half, 1), odd),
    )


def unpack(x_ref, rows_ref):
    chunks = x_ref.shape[2] // lanes

    def step(p, _):
        for m in range(chunks):
            rows_ref[p, m * 16 : (m + 1) * 16, :] = x_ref[
                p, :, m * lanes : (m + 1) * lanes
            ].astype(jnp.float32)
        return 0

    lax.fori_loop(0, x_ref.shape[0], step, 0)


def pack(rows_ref, o_ref):
    chunks = o_ref.shape[2] // lanes

    def step(p, _):
        for m in range(chunks):
            o_ref[p, :, m * lanes : (m + 1) * lanes] = rows_ref[
                p, m * 16 : (m + 1) * 16, :
            ].astype(jnp.bfloat16)
        return 0

    lax.fori_loop(0, o_ref.shape[0], step, 0)


def row_sets(rows_ref, first, split):
    pairs = rows_ref.shape[1] // 16
    if split:
        return [pl.ds(first, pairs, stride=16), pl.ds(first + 8, pairs, stride=16)]
    return [pl.ds(first, pairs, stride=16)]


def gather_matrix(rows_ref, first, split, whole_ref, sides):
    grid_rows, grid_cols = sides
    for r in range(grid_rows):
        for c in range(grid_cols // 2):
            p = r * grid_cols + 2 * c
            sets = row_sets(rows_ref, first, split)
            a = jnp.concatenate([rows_ref[p, s, :] for s in sets], axis=0)
            b = jnp.concatenate([rows_ref[p + 1, s, :] for s in sets], axis=0)
            even, odd = swap_halves(a, b)
            rows = even.shape[0]
            whole_ref[c, pl.ds(2 * rows * r, rows, stride=2), :] = even
            whole_ref[c, pl.ds(2 * rows * r + 1, rows, stride=2), :] = odd
    return jnp.concatenate(
        [whole_ref[c].astype(jnp.bfloat16) for c in range(grid_cols // 2)], axis=1
    )


def scatter_matrix(values, whole_ref, rows_ref, first, split, sides):
    grid_rows, grid_cols = sides
    rows = values.shape[0] // grid_rows // 2
    for c in range(grid_cols // 2):
        whole_ref[c] = values[:, c * lanes : (c + 1) * lanes]
    for r in range(grid_rows):
        for c in range(grid_cols // 2):
            p = r * grid_cols + 2 * c
            even = whole_ref[c, pl.ds(2 * rows * r, rows, stride=2), :]
            odd = whole_ref[c, pl.ds(2 * rows * r + 1, rows, stride=2), :]
            blocks = swap_halves(even, odd)
            sets = row_sets(rows_ref, first, split)
            size = rows // len(sets)
            for n in range(2):
                for k, s in enumerate(sets):
                    rows_ref[p + n, s, :] = blocks[n][k * size : (k + 1) * size]


def forward_kernel(dims, sides, x_ref, o_ref, left_ref, right_ref, rows_in, rows_out, whole, whole2):
    unpack(x_ref, rows_in)

    def step(h, _):
        left = gather_matrix(rows_in, h, False, whole.at[0], sides)
        right = gather_matrix(rows_in, h + 8, False, whole.at[1], sides)
        left_ref[h] = left
        right_ref[h] = right
        scatter_matrix(contract(left, right, *dims), whole2.at[0], rows_out, h, True, sides)
        return 0

    lax.fori_loop(0, left_ref.shape[0], step, 0)
    pack(rows_out, o_ref)


def backward_kernel(
    outgoing, sides, x_ref, left_ref, right_ref, o_ref, rows_in, rows_out, whole, whole2
):
    unpack(x_ref, rows_in)

    def step(h, _):
        grad = gather_matrix(rows_in, h, True, whole.at[0], sides)
        left, right = left_ref[h], right_ref[h]
        if outgoing:
            grad_left, grad_right = contract(grad, right, 1, 0), contract(grad, left, 0, 0)
        else:
            grad_left, grad_right = contract(right, grad, 1, 1), contract(left, grad, 1, 0)
        scatter_matrix(grad_left, whole2.at[0], rows_out, h, False, sides)
        scatter_matrix(grad_right, whole2.at[1], rows_out, h + 8, False, sides)
        return 0

    lax.fori_loop(0, left_ref.shape[0], step, 0)
    pack(rows_out, o_ref)


def triangle_call(body, operands, out_shapes, peers, tokens, big_in, cells):
    wide, narrow = (peers, cells // lanes * 16, lanes), (peers, cells // lanes * 8, lanes)
    vmem = pl.BlockSpec(memory_space=pltpu.VMEM)
    square = pltpu.VMEM((2, tokens // lanes, tokens, lanes), jnp.float32)
    return pl.pallas_call(
        body,
        out_shape=out_shapes,
        in_specs=[vmem] * len(operands),
        out_specs=[vmem] * len(out_shapes),
        scratch_shapes=[
            pltpu.VMEM(wide if big_in else narrow, jnp.float32),
            pltpu.VMEM(narrow if big_in else wide, jnp.float32),
            square,
            square,
        ],
        compiler_params=pltpu.CompilerParams(vmem_limit_bytes=40 << 20),
    )(*operands)


def exchange_kernel(shared, *refs):
    count = len(shared)
    sources, targets = refs[:count], refs[count : 2 * count]
    send_sem, recv_sem, own_sem = refs[2 * count :]
    row, col, cols = lax.axis_index("row"), lax.axis_index("col"), lax.axis_size("col")
    peers = targets[0].shape[0]
    me = row * cols + col

    def device(d):
        q = lax.rem(me + d, peers)
        return q, {"row": q // cols, "col": lax.rem(q, cols)}

    barrier = pltpu.get_barrier_semaphore()
    for d in range(1, peers):
        pl.semaphore_signal(
            barrier, inc=1, device_id=device(d)[1], device_id_type=pl.DeviceIdType.MESH
        )
    pl.semaphore_wait(barrier, peers - 1)
    copies = []
    for n in range(count):
        for d in range(1, peers):
            q, target = device(d)
            copies.append(
                pltpu.make_async_remote_copy(
                    src_ref=sources[n] if shared[n] else sources[n].at[q],
                    dst_ref=targets[n].at[me],
                    send_sem=send_sem.at[n, d],
                    recv_sem=recv_sem.at[n, d],
                    device_id=target,
                    device_id_type=pl.DeviceIdType.MESH,
                )
            )
            copies[-1].start()
        copies.append(
            pltpu.make_async_copy(
                sources[n] if shared[n] else sources[n].at[me], targets[n].at[me], own_sem.at[n]
            )
        )
        copies[-1].start()
    for copy in copies:
        copy.wait()


def exchange_call(number, peers, operands, shared):
    count = len(operands)
    anywhere = pl.BlockSpec(memory_space=pl.ANY)
    outs = [
        jax.ShapeDtypeStruct((peers,) + x.shape[0 if one else 1 :], x.dtype)
        for x, one in zip(operands, shared)
    ]
    return pl.pallas_call(
        functools.partial(exchange_kernel, shared),
        out_shape=outs,
        in_specs=[anywhere] * count,
        out_specs=[anywhere] * count,
        scratch_shapes=[
            pltpu.SemaphoreType.DMA((count, peers)),
            pltpu.SemaphoreType.DMA((count, peers)),
            pltpu.SemaphoreType.DMA((count,)),
        ],
        compiler_params=pltpu.CompilerParams(collective_id=number, has_side_effects=True),
    )(*operands)


def local_mask(tile_mask, chain_ids, row_start, col_start, rows_dev, cols_dev):
    tile_count = tile_mask.shape[0]
    tile_size = chain_ids.shape[0] // tile_count
    row_ids = row_start + jnp.arange(rows_dev, dtype=jnp.int32)
    col_ids = col_start + jnp.arange(cols_dev, dtype=jnp.int32)
    tile_index = jnp.arange(tile_count, dtype=jnp.int32)
    row_hot = (row_ids[:, None] // tile_size == tile_index[None, :]).astype(jnp.float32)
    col_hot = (col_ids[:, None] // tile_size == tile_index[None, :]).astype(jnp.float32)
    tile_vals = jnp.dot(jnp.dot(row_hot, tile_mask.astype(jnp.float32)), col_hot.T)
    row_chain = lax.dynamic_slice_in_dim(chain_ids, row_start, rows_dev)
    col_chain = lax.dynamic_slice_in_dim(chain_ids, col_start, cols_dev)
    same_chain = (row_chain[:, None] == col_chain[None, :]).astype(jnp.float32)
    return jnp.maximum(tile_vals, same_chain).reshape(1, -1)


def per_device(
    pair, cotangent, tile_mask, chain_ids, gain_in, weight_in, weight_gate, gain_out, weight_out
):
    rows_dev, cols_dev, channels = pair.shape
    hidden = weight_out.shape[1]
    grid_rows, grid_cols = lax.axis_size("row"), lax.axis_size("col")
    peers = grid_rows * grid_cols
    share = hidden // peers
    tokens = rows_dev * grid_rows
    cells_dev = rows_dev * cols_dev

    def triangle(spec, a, b):
        return jnp.einsum(spec, a, b, preferred_element_type=jnp.float32)

    numbers = {}

    def exchange(*operands, shared=()):
        shared = shared or (False,) * len(operands)
        if kernels:
            key = (shared,) + tuple(x.shape for x in operands)
            number = numbers.setdefault(key, len(numbers))
            return exchange_call(number, peers, operands, shared)
        return [
            lax.all_to_all(jnp.broadcast_to(x, (peers,) + x.shape) if one else x, axes, 0, 0)
            for x, one in zip(operands, shared)
        ]

    kernels = share == 8 and cols_dev == half and rows_dev == half and grid_cols % 2 == 0
    sides = (grid_rows, grid_cols)
    whole_grid = (share, tokens, tokens)

    def spread(*arrays):
        sent = [a.reshape(peers, share, cells_dev) for a in arrays]
        if len(arrays) == 2 or not kernels:
            return jnp.concatenate(sent, axis=1)
        halves = sent[0].reshape(peers, share, 2, -1).transpose(0, 2, 1, 3)
        return halves.reshape(peers, 2 * share, -1)

    def collect(got, count):
        got = got.astype(jnp.float32)
        if count == 1 and kernels:
            got = got.reshape(peers, 2, share, -1).transpose(0, 2, 1, 3)
            return [got.reshape(hidden, cells_dev)]
        got = got.reshape(peers, count, share, cells_dev)
        return [got[:, n].reshape(hidden, cells_dev) for n in range(count)]

    def assemble(got, count):
        got = got.reshape(grid_rows, grid_cols, count * share, rows_dev, cols_dev)
        whole = got.transpose(2, 0, 3, 1, 4).reshape(count * share, tokens, tokens)
        return [whole[n * share : (n + 1) * share] for n in range(count)]

    def divide(*arrays):
        stacked = jnp.concatenate([a.astype(jnp.bfloat16) for a in arrays], axis=0)
        split = stacked.reshape(-1, grid_rows, rows_dev, grid_cols, cols_dev)
        return split.transpose(1, 3, 0, 2, 4).reshape(peers, -1, cells_dev)

    def shapes(*dims):
        return [jax.ShapeDtypeStruct(d, jnp.bfloat16) for d in dims]

    def forward_triangle(left, right, outgoing):
        (got,) = exchange(spread(left, right))
        if kernels:
            dims = (1, 1) if outgoing else (0, 0)
            blocks, left_all, right_all = triangle_call(
                functools.partial(forward_kernel, dims, sides),
                [got],
                shapes((peers, 16, cells_dev // 2), whole_grid, whole_grid),
                peers,
                tokens,
                True,
                cells_dev,
            )
        else:
            left_all, right_all = assemble(got, 2)
            spec = "hik,hjk->hij" if outgoing else "hki,hkj->hij"
            blocks = divide(triangle(spec, left_all, right_all))
        (got,) = exchange(blocks)
        return collect(got, 1)[0], left_all, right_all

    def backward_triangle(grad, left_all, right_all, outgoing, extra=()):
        got, *parts = exchange(spread(grad), *extra)
        if kernels:
            (blocks,) = triangle_call(
                functools.partial(backward_kernel, outgoing, sides),
                [got, left_all, right_all],
                shapes((peers, 16, cells_dev)),
                peers,
                tokens,
                False,
                cells_dev,
            )
        else:
            (whole,) = assemble(got, 1)
            if outgoing:
                grads = ("hij,hjk->hik", whole, right_all), ("hij,hik->hjk", whole, left_all)
            else:
                grads = ("hkj,hij->hki", right_all, whole), ("hki,hij->hkj", left_all, whole)
            blocks = divide(*[triangle(*g) for g in grads])
        sums = [add_parts(p) for p in parts]
        got, *totals = exchange(blocks, *sums, shared=(False,) + (True,) * len(sums))
        return collect(got, 2) + [t.reshape(-1, hidden) for t in totals]

    factor = 1.0 / tokens

    def stack_parts(weights, gains):
        blocks = [w[:, n : n + hidden] for w in weights for n in range(0, w.shape[1], hidden)]
        rows = jnp.concatenate(blocks + [g[None] for g in gains], axis=0) * factor
        rows = jnp.pad(rows, ((0, -rows.shape[0] % (16 * peers)), (0, 0)))
        return rows.astype(jnp.bfloat16).reshape(peers, -1, hidden)

    def add_parts(parts):
        return jnp.sum(parts.astype(jnp.float32), axis=0).astype(jnp.bfloat16)

    row_start = lax.axis_index("row") * rows_dev
    col_start = lax.axis_index("col") * cols_dev
    pair_mask = local_mask(tile_mask, chain_ids, row_start, col_start, rows_dev, cols_dev)
    cells_one = pair.reshape(-1, channels).T.astype(jnp.float32)
    front_one = front(cells_one, pair_mask, gain_in[0], weight_in[0], weight_gate[0])
    tri_one, left_one, right_one = forward_triangle(front_one[7], front_one[8], True)
    back_one = back_half(cells_one, tri_one, front_one[9], gain_out[0], weight_out[0])
    cells_two = back_one[4].astype(jnp.float32)
    front_two = front(cells_two, pair_mask, gain_in[1], weight_in[1], weight_gate[1])
    tri_two, left_two, right_two = forward_triangle(front_two[7], front_two[8], False)
    back_two = back_half(cells_two, tri_two, front_two[9], gain_out[1], weight_out[1])
    cot_two = cotangent.reshape(-1, channels).T.astype(jnp.float32)
    post_two = post_grad(cot_two, front_two[9], back_two, gain_out[1], weight_out[1])
    dleft_two, dright_two = backward_triangle(post_two[0], left_two, right_two, False)
    pre_two = pre_grad(
        cot_two,
        dleft_two,
        dright_two,
        post_two[1],
        front_two,
        pair_mask,
        gain_in[1],
        weight_in[1],
        weight_gate[1],
    )
    cot_one = pre_two[0].astype(jnp.bfloat16).astype(jnp.float32)
    post_one = post_grad(cot_one, front_one[9], back_one, gain_out[0], weight_out[0])
    early = stack_parts(
        (pre_two[1], pre_two[2], post_two[2], post_one[2]), (pre_two[3], post_two[3], post_one[3])
    )
    dleft_one, dright_one, early = backward_triangle(
        post_one[0], left_one, right_one, True, (early,)
    )
    pre_one = pre_grad(
        cot_one,
        dleft_one,
        dright_one,
        post_one[1],
        front_one,
        pair_mask,
        gain_in[0],
        weight_in[0],
        weight_gate[0],
    )
    grad_pair = pre_one[0].astype(jnp.bfloat16).T.reshape(rows_dev, cols_dev, channels)

    (parts,) = exchange(stack_parts((pre_one[1], pre_one[2]), (pre_one[3],)))
    (late,) = exchange(add_parts(parts), shared=(True,))
    early = early.astype(jnp.float32)
    late = late.reshape(-1, hidden).astype(jnp.float32)

    def block(rows, n, count=1):
        blocks = rows[n * channels : (n + count) * channels].reshape(count, channels, hidden)
        return jnp.concatenate([blocks[k] for k in range(count)], axis=1)

    return (
        grad_pair,
        jnp.stack([block(late, 0, 4), block(early, 0, 4)]),
        jnp.stack([block(late, 4), block(early, 4)]),
        jnp.stack([block(early, 6), block(early, 5)]),
        jnp.stack([late[5 * channels], early[7 * channels]]),
        jnp.stack([early[7 * channels + 2], early[7 * channels + 1]]),
    )


def solution(mesh):
    in_specs = (
        P(("grp", "row"), "col", None),
        P(("grp", "row"), "col", None),
        P("grp", None),
        P("grp"),
        P(),
        P(),
        P(),
        P(),
        P(),
    )
    out_specs = (
        P(("grp", "row"), "col", None),
        P("grp", None, None),
        P("grp", None, None),
        P("grp", None, None),
        P("grp", None),
        P("grp", None),
    )
    return jax.shard_map(
        per_device, mesh=mesh, in_specs=in_specs, out_specs=out_specs, check_vma=False
    )
```

```python
import functools

import jax
import jax.numpy as jnp
from jax import lax
from jax.experimental import pallas as pl
from jax.experimental.pallas import tpu as pltpu
from jax.sharding import PartitionSpec as P

eps = 1e-05
axes = ("row", "col")


def contract(a, b, dim_a, dim_b):
    return lax.dot_general(a, b, (((dim_a,), (dim_b,)), ((), ())), preferred_element_type=jnp.float32)


def layer_normalize(values):
    average = jnp.mean(values, axis=0, keepdims=True)
    centred = values - average
    inv_std = lax.rsqrt(jnp.mean(centred * centred, axis=0, keepdims=True) + eps)
    return (centred * inv_std, inv_std)


def norm_backward_step(grad_hat, normed, inv_std):
    inner = jnp.mean(grad_hat * normed, axis=0, keepdims=True)
    return inv_std * (grad_hat - jnp.mean(grad_hat, axis=0, keepdims=True) - normed * inner)


def front(cells, pair_mask, gain, weight_proj, weight_gating):
    zhat, inv_std = layer_normalize(cells)
    znorm = (zhat * gain[:, None]).astype(jnp.bfloat16)
    projected = contract(weight_proj, znorm, 0, 0)
    width = weight_proj.shape[1] // 4
    left_lin = projected[:width]
    left_gate = jax.nn.sigmoid(projected[width : 2 * width])
    right_lin = projected[2 * width : 3 * width]
    right_gate = jax.nn.sigmoid(projected[3 * width :])
    left = (pair_mask * left_gate * left_lin).astype(jnp.bfloat16)
    right = (right_gate * right_lin).astype(jnp.bfloat16)
    gating = jax.nn.sigmoid(contract(weight_gating, znorm, 0, 0))
    return (zhat, inv_std, znorm, left_lin, left_gate, right_lin, right_gate, left, right, gating)


def back_half(cells, tri, gating, gain, weight_final):
    xhat, inv_std = layer_normalize(tri)
    xnorm = (xhat * gain[:, None]).astype(jnp.bfloat16)
    update = contract(weight_final, xnorm, 0, 0)
    result = (cells + gating * update).astype(jnp.bfloat16)
    return (xhat, inv_std, xnorm, update, result)


def post_grad(incoming, gating, backs, gain, weight_final):
    xhat, inv_std, xnorm, update = backs[:4]
    grad_update = (incoming * gating).astype(jnp.bfloat16)
    grad_gating = (incoming * update * gating * (1.0 - gating)).astype(jnp.bfloat16)
    grad_wout = contract(xnorm, grad_update, 1, 1)
    grad_xnorm = contract(weight_final, grad_update, 1, 0)
    grad_gout = jnp.sum(grad_xnorm * xhat, axis=1)
    grad_tri = norm_backward_step(grad_xnorm * gain[:, None], xhat, inv_std).astype(jnp.bfloat16)
    return (grad_tri, grad_gating, grad_wout, grad_gout)


def pre_grad(
    incoming, grad_left, grad_right, grad_gating, fronts, pair_mask, gain, weight_proj, weight_gating
):
    zhat, inv_std, znorm, left_lin, left_gate, right_lin, right_gate = fronts[:7]
    masked = grad_left * pair_mask
    grad_proj = jnp.concatenate(
        [
            masked * left_gate,
            masked * left_lin * left_gate * (1.0 - left_gate),
            grad_right * right_gate,
            grad_right * right_lin * right_gate * (1.0 - right_gate),
        ],
        axis=0,
    ).astype(jnp.bfloat16)
    grad_win = contract(znorm, grad_proj, 1, 1)
    grad_wgate = contract(znorm, grad_gating, 1, 1)
    grad_znorm = contract(weight_proj, grad_proj, 1, 0)
    grad_znorm = grad_znorm + contract(weight_gating, grad_gating, 1, 0)
    grad_gin = jnp.sum(grad_znorm * zhat, axis=1)
    grad_input = incoming + norm_backward_step(grad_znorm * gain[:, None], zhat, inv_std)
    return (grad_input, grad_win, grad_wgate, grad_gin)


lanes = 128
half = lanes // 2


def swap_halves(even, odd):
    low = lax.broadcasted_iota(jnp.int32, even.shape, 1) < half
    return (
        jnp.where(low, even, pltpu.roll(odd, half, 1)),
        jnp.where(low, pltpu.roll(even, half, 1), odd),
    )


def unpack(x_ref, rows_ref):
    chunks = x_ref.shape[2] // lanes

    def step(p, _):
        for m in range(chunks):
            rows_ref[p, m * 16 : (m + 1) * 16, :] = x_ref[
                p, :, m * lanes : (m + 1) * lanes
            ].astype(jnp.float32)
        return 0

    lax.fori_loop(0, x_ref.shape[0], step, 0)


def pack(rows_ref, o_ref):
    chunks = o_ref.shape[2] // lanes

    def step(p, _):
        for m in range(chunks):
            o_ref[p, :, m * lanes : (m + 1) * lanes] = rows_ref[
                p, m * 16 : (m + 1) * 16, :
            ].astype(jnp.bfloat16)
        return 0

    lax.fori_loop(0, o_ref.shape[0], step, 0)


def row_sets(rows_ref, first, split):
    pairs = rows_ref.shape[1] // 16
    if split:
        return [pl.ds(first, pairs, stride=16), pl.ds(first + 8, pairs, stride=16)]
    return [pl.ds(first, pairs, stride=16)]


def gather_matrix(rows_ref, first, split, whole_ref, sides):
    grid_rows, grid_cols = sides
    for r in range(grid_rows):
        for c in range(grid_cols // 2):
            p = r * grid_cols + 2 * c
            sets = row_sets(rows_ref, first, split)
            a = jnp.concatenate([rows_ref[p, s, :] for s in sets], axis=0)
            b = jnp.concatenate([rows_ref[p + 1, s, :] for s in sets], axis=0)
            even, odd = swap_halves(a, b)
            rows = even.shape[0]
            whole_ref[c, pl.ds(2 * rows * r, rows, stride=2), :] = even
            whole_ref[c, pl.ds(2 * rows * r + 1, rows, stride=2), :] = odd
    return jnp.concatenate(
        [whole_ref[c].astype(jnp.bfloat16) for c in range(grid_cols // 2)], axis=1
    )


def scatter_matrix(values, whole_ref, rows_ref, first, split, sides):
    grid_rows, grid_cols = sides
    rows = values.shape[0] // grid_rows // 2
    for c in range(grid_cols // 2):
        whole_ref[c] = values[:, c * lanes : (c + 1) * lanes]
    for r in range(grid_rows):
        for c in range(grid_cols // 2):
            p = r * grid_cols + 2 * c
            even = whole_ref[c, pl.ds(2 * rows * r, rows, stride=2), :]
            odd = whole_ref[c, pl.ds(2 * rows * r + 1, rows, stride=2), :]
            blocks = swap_halves(even, odd)
            sets = row_sets(rows_ref, first, split)
            size = rows // len(sets)
            for n in range(2):
                for k, s in enumerate(sets):
                    rows_ref[p + n, s, :] = blocks[n][k * size : (k + 1) * size]


def forward_kernel(dims, sides, x_ref, o_ref, left_ref, right_ref, rows_in, rows_out, whole, whole2):
    unpack(x_ref, rows_in)

    def step(h, _):
        left = gather_matrix(rows_in, h, False, whole.at[0], sides)
        right = gather_matrix(rows_in, h + 8, False, whole.at[1], sides)
        left_ref[h] = left
        right_ref[h] = right
        scatter_matrix(contract(left, right, *dims), whole2.at[0], rows_out, h, True, sides)
        return 0

    lax.fori_loop(0, left_ref.shape[0], step, 0)
    pack(rows_out, o_ref)


def backward_kernel(
    outgoing, sides, x_ref, left_ref, right_ref, o_ref, rows_in, rows_out, whole, whole2
):
    unpack(x_ref, rows_in)

    def step(h, _):
        grad = gather_matrix(rows_in, h, True, whole.at[0], sides)
        left, right = left_ref[h], right_ref[h]
        if outgoing:
            grad_left, grad_right = contract(grad, right, 1, 0), contract(grad, left, 0, 0)
        else:
            grad_left, grad_right = contract(right, grad, 1, 1), contract(left, grad, 1, 0)
        scatter_matrix(grad_left, whole2.at[0], rows_out, h, False, sides)
        scatter_matrix(grad_right, whole2.at[1], rows_out, h + 8, False, sides)
        return 0

    lax.fori_loop(0, left_ref.shape[0], step, 0)
    pack(rows_out, o_ref)


def triangle_call(body, operands, out_shapes, peers, tokens, big_in, cells):
    wide, narrow = (peers, cells // lanes * 16, lanes), (peers, cells // lanes * 8, lanes)
    vmem = pl.BlockSpec(memory_space=pltpu.VMEM)
    square = pltpu.VMEM((2, tokens // lanes, tokens, lanes), jnp.float32)
    return pl.pallas_call(
        body,
        out_shape=out_shapes,
        in_specs=[vmem] * len(operands),
        out_specs=[vmem] * len(out_shapes),
        scratch_shapes=[
            pltpu.VMEM(wide if big_in else narrow, jnp.float32),
            pltpu.VMEM(narrow if big_in else wide, jnp.float32),
            square,
            square,
        ],
        compiler_params=pltpu.CompilerParams(vmem_limit_bytes=40 << 20),
    )(*operands)


def exchange_kernel(shared, *refs):
    count = len(shared)
    sources, targets = refs[:count], refs[count : 2 * count]
    send_sem, recv_sem, own_sem = refs[2 * count :]
    row, col, cols = lax.axis_index("row"), lax.axis_index("col"), lax.axis_size("col")
    peers = targets[0].shape[0]
    me = row * cols + col

    def device(d):
        q = lax.rem(me + d, peers)
        return q, {"row": q // cols, "col": lax.rem(q, cols)}

    barrier = pltpu.get_barrier_semaphore()
    for d in range(1, peers):
        pl.semaphore_signal(
            barrier, inc=1, device_id=device(d)[1], device_id_type=pl.DeviceIdType.MESH
        )
    pl.semaphore_wait(barrier, peers - 1)
    copies = []
    for n in range(count):
        for d in range(1, peers):
            q, target = device(d)
            copies.append(
                pltpu.make_async_remote_copy(
                    src_ref=sources[n] if shared[n] else sources[n].at[q],
                    dst_ref=targets[n].at[me],
                    send_sem=send_sem.at[n, d],
                    recv_sem=recv_sem.at[n, d],
                    device_id=target,
                    device_id_type=pl.DeviceIdType.MESH,
                )
            )
            copies[-1].start()
        copies.append(
            pltpu.make_async_copy(
                sources[n] if shared[n] else sources[n].at[me], targets[n].at[me], own_sem.at[n]
            )
        )
        copies[-1].start()
    for copy in copies:
        copy.wait()


def exchange_call(number, peers, operands, shared):
    count = len(operands)
    anywhere = pl.BlockSpec(memory_space=pl.ANY)
    outs = [
        jax.ShapeDtypeStruct((peers,) + x.shape[0 if one else 1 :], x.dtype)
        for x, one in zip(operands, shared)
    ]
    return pl.pallas_call(
        functools.partial(exchange_kernel, shared),
        out_shape=outs,
        in_specs=[anywhere] * count,
        out_specs=[anywhere] * count,
        scratch_shapes=[
            pltpu.SemaphoreType.DMA((count, peers)),
            pltpu.SemaphoreType.DMA((count, peers)),
            pltpu.SemaphoreType.DMA((count,)),
        ],
        compiler_params=pltpu.CompilerParams(collective_id=number, has_side_effects=True),
    )(*operands)


def local_mask(tile_mask, chain_ids, row_start, col_start, rows_dev, cols_dev):
    tile_count = tile_mask.shape[0]
    tile_size = chain_ids.shape[0] // tile_count
    row_ids = row_start + jnp.arange(rows_dev, dtype=jnp.int32)
    col_ids = col_start + jnp.arange(cols_dev, dtype=jnp.int32)
    tile_index = jnp.arange(tile_count, dtype=jnp.int32)
    row_hot = (row_ids[:, None] // tile_size == tile_index[None, :]).astype(jnp.float32)
    col_hot = (col_ids[:, None] // tile_size == tile_index[None, :]).astype(jnp.float32)
    tile_vals = jnp.dot(jnp.dot(row_hot, tile_mask.astype(jnp.float32)), col_hot.T)
    row_chain = lax.dynamic_slice_in_dim(chain_ids, row_start, rows_dev)
    col_chain = lax.dynamic_slice_in_dim(chain_ids, col_start, cols_dev)
    same_chain = (row_chain[:, None] == col_chain[None, :]).astype(jnp.float32)
    return jnp.maximum(tile_vals, same_chain).reshape(1, -1)


def per_device(
    pair, cotangent, tile_mask, chain_ids, gain_in, weight_in, weight_gate, gain_out, weight_out
):
    rows_dev, cols_dev, channels = pair.shape
    hidden = weight_out.shape[1]
    grid_rows, grid_cols = lax.axis_size("row"), lax.axis_size("col")
    peers = grid_rows * grid_cols
    share = hidden // peers
    tokens = rows_dev * grid_rows
    cells_dev = rows_dev * cols_dev

    def triangle(spec, a, b):
        return jnp.einsum(spec, a, b, preferred_element_type=jnp.float32)

    numbers = {}

    def exchange(*operands, shared=(), direct=True):
        shared = shared or (False,) * len(operands)
        if kernels and direct:
            key = (shared,) + tuple(x.shape for x in operands)
            number = numbers.setdefault(key, len(numbers))
            return exchange_call(number, peers, operands, shared)
        return [
            lax.all_to_all(jnp.broadcast_to(x, (peers,) + x.shape) if one else x, axes, 0, 0)
            for x, one in zip(operands, shared)
        ]

    kernels = share == 8 and cols_dev == half and rows_dev == half and grid_cols % 2 == 0
    sides = (grid_rows, grid_cols)
    whole_grid = (share, tokens, tokens)

    def spread(*arrays):
        sent = [a.reshape(peers, share, cells_dev) for a in arrays]
        if len(arrays) == 2 or not kernels:
            return jnp.concatenate(sent, axis=1)
        halves = sent[0].reshape(peers, share, 2, -1).transpose(0, 2, 1, 3)
        return halves.reshape(peers, 2 * share, -1)

    def collect(got, count):
        if count == 1 and kernels:
            got = got.reshape(peers, 2, share, -1).transpose(0, 2, 1, 3)
            return [got.reshape(hidden, cells_dev).astype(jnp.float32)]
        got = got.reshape(peers, count, share, cells_dev)
        return [
            got[:, n].reshape(hidden, cells_dev).astype(jnp.float32) for n in range(count)
        ]

    def assemble(got, count):
        got = got.reshape(grid_rows, grid_cols, count * share, rows_dev, cols_dev)
        whole = got.transpose(2, 0, 3, 1, 4).reshape(count * share, tokens, tokens)
        return [whole[n * share : (n + 1) * share] for n in range(count)]

    def divide(*arrays):
        stacked = jnp.concatenate([a.astype(jnp.bfloat16) for a in arrays], axis=0)
        split = stacked.reshape(-1, grid_rows, rows_dev, grid_cols, cols_dev)
        return split.transpose(1, 3, 0, 2, 4).reshape(peers, -1, cells_dev)

    def shapes(*dims):
        return [jax.ShapeDtypeStruct(d, jnp.bfloat16) for d in dims]

    def forward_triangle(left, right, outgoing):
        (got,) = exchange(spread(left, right))
        if kernels:
            dims = (1, 1) if outgoing else (0, 0)
            blocks, left_all, right_all = triangle_call(
                functools.partial(forward_kernel, dims, sides),
                [got],
                shapes((peers, 16, cells_dev // 2), whole_grid, whole_grid),
                peers,
                tokens,
                True,
                cells_dev,
            )
        else:
            left_all, right_all = assemble(got, 2)
            spec = "hik,hjk->hij" if outgoing else "hki,hkj->hij"
            blocks = divide(triangle(spec, left_all, right_all))
        (got,) = exchange(blocks, direct=False)
        return collect(got, 1)[0], left_all, right_all

    def backward_triangle(grad, left_all, right_all, outgoing):
        (got,) = exchange(spread(grad))
        if kernels:
            (blocks,) = triangle_call(
                functools.partial(backward_kernel, outgoing, sides),
                [got, left_all, right_all],
                shapes((peers, 16, cells_dev)),
                peers,
                tokens,
                False,
                cells_dev,
            )
        else:
            (whole,) = assemble(got, 1)
            if outgoing:
                grads = ("hij,hjk->hik", whole, right_all), ("hij,hik->hjk", whole, left_all)
            else:
                grads = ("hkj,hij->hki", right_all, whole), ("hki,hij->hkj", left_all, whole)
            blocks = divide(*[triangle(*g) for g in grads])
        (got,) = exchange(blocks, direct=False)
        return collect(got, 2)

    factor = 1.0 / tokens

    def stack_parts(weights, gains):
        blocks = [w[:, n : n + hidden] for w in weights for n in range(0, w.shape[1], hidden)]
        rows = jnp.concatenate(blocks + [g[None] for g in gains], axis=0) * factor
        rows = jnp.pad(rows, ((0, -rows.shape[0] % peers), (0, 0)))
        return rows.astype(jnp.bfloat16).reshape(peers, -1, hidden)

    def add_parts(parts):
        return jnp.sum(parts.astype(jnp.float32), axis=0).astype(jnp.bfloat16)

    row_start = lax.axis_index("row") * rows_dev
    col_start = lax.axis_index("col") * cols_dev
    pair_mask = local_mask(tile_mask, chain_ids, row_start, col_start, rows_dev, cols_dev)
    cells_one = pair.reshape(-1, channels).T.astype(jnp.float32)
    front_one = front(cells_one, pair_mask, gain_in[0], weight_in[0], weight_gate[0])
    tri_one, left_one, right_one = forward_triangle(front_one[7], front_one[8], True)
    back_one = back_half(cells_one, tri_one, front_one[9], gain_out[0], weight_out[0])
    cells_two = back_one[4].astype(jnp.float32)
    front_two = front(cells_two, pair_mask, gain_in[1], weight_in[1], weight_gate[1])
    tri_two, left_two, right_two = forward_triangle(front_two[7], front_two[8], False)
    back_two = back_half(cells_two, tri_two, front_two[9], gain_out[1], weight_out[1])
    cot_two = cotangent.reshape(-1, channels).T.astype(jnp.float32)
    post_two = post_grad(cot_two, front_two[9], back_two, gain_out[1], weight_out[1])
    dleft_two, dright_two = backward_triangle(post_two[0], left_two, right_two, False)
    pre_two = pre_grad(
        cot_two,
        dleft_two,
        dright_two,
        post_two[1],
        front_two,
        pair_mask,
        gain_in[1],
        weight_in[1],
        weight_gate[1],
    )
    cot_one = pre_two[0].astype(jnp.bfloat16).astype(jnp.float32)
    post_one = post_grad(cot_one, front_one[9], back_one, gain_out[0], weight_out[0])
    dleft_one, dright_one = backward_triangle(post_one[0], left_one, right_one, True)
    pre_one = pre_grad(
        cot_one,
        dleft_one,
        dright_one,
        post_one[1],
        front_one,
        pair_mask,
        gain_in[0],
        weight_in[0],
        weight_gate[0],
    )
    grad_pair = pre_one[0].astype(jnp.bfloat16).T.reshape(rows_dev, cols_dev, channels)

    stacked = stack_parts(
        (pre_one[1], pre_one[2], post_one[2], pre_two[1], pre_two[2], post_two[2]),
        (pre_one[3], pre_two[3], post_one[3], post_two[3]),
    )
    (parts,) = exchange(stacked, direct=False)
    (totals,) = exchange(add_parts(parts), shared=(True,), direct=False)
    totals = totals.reshape(-1, hidden).astype(jnp.float32)
    blocks = totals[: 12 * channels].reshape(2, 6, channels, hidden)
    gains = totals[12 * channels :]
    return (
        grad_pair,
        jnp.concatenate([blocks[:, n] for n in range(4)], axis=2),
        blocks[:, 4],
        blocks[:, 5],
        gains[:2],
        gains[2:4],
    )


def solution(mesh):
    in_specs = (
        P(("grp", "row"), "col", None),
        P(("grp", "row"), "col", None),
        P("grp", None),
        P("grp"),
        P(),
        P(),
        P(),
        P(),
        P(),
    )
    out_specs = (
        P(("grp", "row"), "col", None),
        P("grp", None, None),
        P("grp", None, None),
        P("grp", None, None),
        P("grp", None),
        P("grp", None),
    )
    return jax.shard_map(
        per_device, mesh=mesh, in_specs=in_specs, out_specs=out_specs, check_vma=False
    )
```
